32 devices in a mesh: groups: 2 (over x), tm: 8 (over z, y), state: 2 (over core).
Axes of the slice: x: 2, y: 2, z: 4, core: 2. Of those that a mesh axis runs over, the one named last changes fastest.
Arguments:
- observed: int32 [512], P(('groups', 'tm')), parts along dimension 0, may hold values from 0 to 255
- block_mask: int32 [64, 64], replicated, may hold values 0 or 1
- jump_logit: float32 [512, 512], replicated, may hold values from -4 to 4
- leave_rate: float32 [512], replicated, may hold values from 0.0003 to 0.05
- emit_logit: float32 [256, 512], replicated, may hold values from -3.95 to 4.55
- prior_logit: float32 [512], replicated, may hold values from -4 to 4
Outputs:
- marginals: float32 [512, 512], P(('groups', 'tm'), 'state'), parts along dimension 0
The draws below stay inside these ranges and needn't reach their ends.
There are 2 independent parts, one for each index of `groups`. The reference program is written for one: setup_inputs(seed, part) draws one part's arguments, and reference() takes and returns one part's arrays. A program takes and returns all parts, laid end to end along the dimension named above; an argument that names none is the same for every part. Nothing has to cross between parts.
All inputs are finite; a program needn't handle non-finite values.
Results may differ from the reference program's by a relative error of at most 0.0003.
Values sent between devices are 32-bit elements; how exact they have to be, the bound alone decides.
A program may use at most 64 MiB of HBM per device.

```python
import math
import jax
import jax.numpy as jnp
from jax import lax

S = 512
V = 256
NB = 64
TIME = 256


def draw_observed(key, part):
    key = jax.random.fold_in(key, 23)
    start_key, regime_key, class_key, member_key = jax.random.split(key, 4)
    starts = (jax.random.randint(start_key, (TIME,), 0, 12) == 0).astype(jnp.int32)
    segment = jnp.cumsum(starts).astype(jnp.int32)
    regime = jax.random.randint(regime_key, (TIME + 1,), 0, 4)
    loudness = jax.random.randint(class_key, (TIME + 1,), 0, 2)
    member = jax.random.randint(member_key, (TIME,), 0, V // 8)
    symbols = jnp.take(regime, segment) + 4 * jnp.take(loudness, segment) + 8 * member
    return symbols.astype(jnp.int32)


def draw_emit_logit(key, part):
    key = jax.random.fold_in(key, 11)
    symbol_ids = jnp.arange(V, dtype=jnp.int32)
    state_ids = jnp.arange(S, dtype=jnp.int32)
    symbol_regime = symbol_ids % 4
    symbol_class = symbol_ids // 4 % 2
    state_regime = state_ids // (S // NB) % 4
    matching = (symbol_regime[:, None] == state_regime[None, :]).astype(jnp.float32)
    loud = 3.0
    match_gain = 0.5
    noise = jnp.clip(0.3 * jax.random.normal(key, (V, S), jnp.float32), -0.9, 0.9)
    offset = jnp.where(symbol_class == 0, loud, -loud).astype(jnp.float32)
    return (offset[:, None] + match_gain * matching + noise).astype(jnp.float32)


def touch_ends(array, rng, low, largest):
    place = [jax.random.randint(jax.random.fold_in(rng, axis), (), 0, length) for axis, length in enumerate(array.shape)]
    widest = array.shape.index(max(array.shape))
    neighbour = place[:widest] + [(place[widest] + 1) % array.shape[widest]] + place[widest + 1:]
    return array.at[tuple(place)].set(low).at[tuple(neighbour)].set(largest)


def normal_values(own_key, dims, spread, bound, kind=jnp.bfloat16):
    return jnp.clip(spread * jax.random.normal(own_key, dims, jnp.float32), -bound, bound).astype(kind)


def setup_inputs(seed: int = 0, part: int = 0) -> dict:
    key_of = jax.random.split(jax.random.key(seed), 7)
    own_keys = jax.random.split(jax.random.fold_in(key_of[6], part), 7)
    observed = draw_observed(jax.random.fold_in(jax.random.fold_in(key_of[6], part), 71), part)
    block_mask = touch_ends((jax.random.randint(key_of[1], (NB, NB), 0, 4) < 1).astype(jnp.int32), jax.random.fold_in(key_of[1], 1), 0, 1)
    jump_logit = normal_values(key_of[2], (S, S), 1.0, 4.0, jnp.float32)
    leave_rate = jnp.clip(jnp.exp(jax.random.uniform(key_of[3], (S,), jnp.float32, math.log(0.0003), math.log(0.05))), 0.0003, 0.05)
    emit_logit = draw_emit_logit(jax.random.fold_in(key_of[6], 71), part)
    prior_logit = normal_values(key_of[5], (S,), 1.0, 4.0, jnp.float32)
    return dict(observed=observed, block_mask=block_mask, jump_logit=jump_logit, leave_rate=leave_rate, emit_logit=emit_logit, prior_logit=prior_logit)


exact_mode = lax.Precision.HIGHEST


def build_model(block_mask, jump_logit, leave_rate, emit_logit, prior_logit):
    state_count = jump_logit.shape[0]
    block_width = state_count // block_mask.shape[0]
    block_grid = jnp.repeat(jnp.repeat(block_mask, block_width, axis=0), block_width, axis=1)
    block_ids = jnp.arange(state_count, dtype=jnp.int32) // block_width
    diagonal_blocks = (block_ids[:, None] == block_ids[None, :]).astype(jnp.int32)
    allowed = jnp.maximum(block_grid, diagonal_blocks)
    weights = jnp.where(allowed > 0, jnp.exp(jump_logit), 0.0)
    jump_matrix = weights / jnp.sum(weights, axis=1, keepdims=True)
    staying = jnp.eye(state_count, dtype=jump_logit.dtype) * (1.0 - leave_rate)[:, None]
    transition = staying + leave_rate[:, None] * jump_matrix
    emit_weight = jnp.exp(emit_logit)
    emission = emit_weight / jnp.sum(emit_weight, axis=0, keepdims=True)
    prior_weight = jnp.exp(prior_logit)
    initial_dist = prior_weight / jnp.sum(prior_weight)
    return transition, emission, initial_dist


def forward_backward(transition, likelihood, opening, closing):
    def forward_step(state_vec, emitted):
        advanced = jnp.dot(state_vec, transition, precision=exact_mode) * emitted
        advanced = advanced / jnp.sum(advanced)
        return advanced, advanced

    def backward_step(state_vec, emitted):
        previous = jnp.dot(transition, emitted * state_vec, precision=exact_mode)
        previous = previous / jnp.sum(previous)
        return previous, state_vec

    unused, alphas = lax.scan(forward_step, opening, likelihood)
    first_beta, later_betas = lax.scan(backward_step, closing, likelihood[1:], reverse=True)
    beta_rows = jnp.concatenate([first_beta[None, :], later_betas], axis=0)
    posterior = alphas * beta_rows
    return posterior * (transition.shape[0] / jnp.sum(posterior, axis=1, keepdims=True))


def reference(observed, block_mask, jump_logit, leave_rate, emit_logit, prior_logit):
    transition, emission, initial_dist = build_model(block_mask, jump_logit, leave_rate, emit_logit, prior_logit)
    likelihood = jnp.take(emission, observed, axis=0)
    closing = jnp.ones((transition.shape[0],), jnp.float32)
    return forward_backward(transition, likelihood, initial_dist, closing)
```

```python
import functools

import jax
import jax.numpy as jnp
from jax import lax
from jax.experimental import pallas as pl
from jax.experimental.pallas import tpu as pltpu
from jax.sharding import PartitionSpec as P

MESH = pl.DeviceIdType.MESH
F32 = jnp.float32
BF16 = jnp.bfloat16
CHUNKS = 2


def split(x):
    high = x.astype(BF16).astype(F32)
    return high, x - high


def pair(x):
    high, low = split(x)
    row = lax.broadcasted_iota(jnp.int32, (16, x.shape[1]), 0)
    return jnp.where(row == 0, high, jnp.where(row == 1, low, 0.0)).astype(BF16)


def times(x, weights):
    out = jnp.dot(pair(x), weights, preferred_element_type=F32)
    n = out.shape[1] // 2
    return (out[0:1, :n] + out[1:2, :n]) + (out[0:1, n:] + out[1:2, n:])


def put_pieces(ref, x):
    high, low = split(x)
    n = x.shape[1]
    ref[:, :n] = high.astype(BF16)
    ref[:, n:] = low.astype(BF16)


def kernel(
    shard_count,
    observed_ref, mask_ref, jump_ref, leave_ref, emit_ref, prior_ref,
    out_ref,
    moves, fwd_w, bwd_w, symbols, lik, part, logs, chain_f, chain_b,
    peak_out, peak_in, fwd_out, fwd_in, bwd_out, bwd_in, alphas, betas,
    peak_sems, fwd_send, fwd_recv, bwd_send, bwd_recv,
):
    shard = lax.axis_index("tm")
    core = lax.axis_index("state")
    states = jump_ref.shape[0]
    half = states // 2
    steps = lik.shape[0]
    first, last = shard == 0, shard == shard_count - 1

    barrier = pltpu.get_barrier_semaphore()
    pl.semaphore_signal(barrier, inc=1, device_id={"state": 1 - core}, device_id_type=MESH)

    @pl.when(jnp.logical_not(first))
    def _():
        for c in range(2):
            pl.semaphore_signal(
                barrier, inc=1, device_id={"tm": shard - 1, "state": c}, device_id_type=MESH
            )

    @pl.when(jnp.logical_not(last))
    def _():
        for c in range(2):
            pl.semaphore_signal(
                barrier, inc=1, device_id={"tm": shard + 1, "state": c}, device_id_type=MESH
            )

    width = states // mask_ref.shape[0]
    blocks = mask_ref.shape[0]
    spread = (
        lax.broadcasted_iota(jnp.int32, (states, blocks), 0) // width
        == lax.broadcasted_iota(jnp.int32, (states, blocks), 1)
    ).astype(F32).astype(BF16)
    spread_t = (
        lax.broadcasted_iota(jnp.int32, (blocks, states), 1) // width
        == lax.broadcasted_iota(jnp.int32, (blocks, states), 0)
    ).astype(F32).astype(BF16)
    eye = lax.broadcasted_iota(jnp.int32, (blocks, blocks), 0) == lax.broadcasted_iota(
        jnp.int32, (blocks, blocks), 1
    )
    grid = jnp.where(eye, 1.0, mask_ref[...].astype(F32)).astype(BF16)
    tall = jnp.dot(spread, grid, preferred_element_type=F32).astype(BF16)
    allowed = jnp.dot(tall, spread_t, preferred_element_type=F32)
    weights = jnp.where(allowed > 0.5, jnp.exp(jump_ref[...]), 0.0)
    leave = leave_ref[...]
    stay = 1.0 - leave
    leave_col = jnp.transpose(jnp.broadcast_to(leave, (128, states)))[:, 0:1]
    off = weights * (leave_col / jnp.sum(weights, axis=1, keepdims=True))
    moves[...] = off
    put_pieces(fwd_w, off)
    put_pieces(bwd_w, jnp.transpose(off))

    emit = jnp.exp(emit_ref[...])
    symbols[...] = emit
    share = 1.0 / jnp.sum(emit, axis=0, keepdims=True)
    for t in range(steps):
        lik[t:t + 1, :] = symbols[pl.ds(observed_ref[t], 1), :]
    rows = lik[...] * share
    lik[...] = rows / jnp.max(rows, axis=1, keepdims=True)

    own = lax.broadcasted_iota(jnp.int32, (half, states), 0) + core * half
    diagonal = own == lax.broadcasted_iota(jnp.int32, (half, states), 1)
    start = pl.multiple_of(core * half, half)
    part[...] = (moves[pl.ds(start, half), :] + jnp.where(diagonal, stay, 0.0)) * lik[0:1, :]
    logs[...] = jnp.zeros_like(logs)
    size = half // CHUNKS

    def advance(t, rescale):
        emitted = lik[pl.ds(t, 1), :]
        for h in range(CHUNKS):
            at = slice(h * size, (h + 1) * size)
            a = part[at, :]
            high, low = split(a)
            high, low = high.astype(BF16), low.astype(BF16)
            both = jnp.dot(
                jnp.concatenate([high, low], axis=0), fwd_w[:, :states],
                preferred_element_type=F32,
            )
            rest = jnp.dot(high, fwd_w[:, states:], preferred_element_type=F32)
            new = (a * stay + (both[:size] + (both[size:] + rest))) * emitted
            if rescale:
                peak = jnp.max(a, axis=1, keepdims=True)
                new = new * (1.0 / peak)
                logs[at, :] = logs[at, :] + jnp.log(peak)
            part[at, :] = new

    def two(i, carry):
        advance(1 + 2 * i, True)
        advance(2 + 2 * i, False)
        return carry

    lax.fori_loop(0, (steps - 1) // 2, two, 0)
    if (steps - 1) % 2:
        advance(steps - 1, True)

    final_log = logs[...]
    own_peak = jnp.max(final_log + jnp.log(jnp.max(part[...], axis=1, keepdims=True)))
    peak_out[...] = jnp.full(peak_out.shape, own_peak, F32)
    neighbours = 1 + 2 * (
        jnp.where(first, 0, 1).astype(jnp.int32) + jnp.where(last, 0, 1).astype(jnp.int32)
    )
    pl.semaphore_wait(barrier, neighbours)
    peak_copy = pltpu.make_async_remote_copy(
        src_ref=peak_out, dst_ref=peak_in, send_sem=peak_sems.at[0], recv_sem=peak_sems.at[1],
        device_id={"state": 1 - core}, device_id_type=MESH,
    )
    peak_copy.start()
    peak_copy.wait()
    top = jnp.maximum(peak_out[0:1, 0:1], peak_in[0:1, 0:1])
    whole = part[...] * jnp.exp(final_log - top)
    put_pieces(chain_f, whole)
    put_pieces(chain_b, jnp.transpose(whole))

    def fwd_copy(c):
        return pltpu.make_async_remote_copy(
            src_ref=fwd_out, dst_ref=fwd_in.at[core],
            send_sem=fwd_send.at[c], recv_sem=fwd_recv.at[core],
            device_id={"tm": shard + 1, "state": c}, device_id_type=MESH,
        )

    def bwd_copy(c):
        return pltpu.make_async_remote_copy(
            src_ref=bwd_out, dst_ref=bwd_in.at[core],
            send_sem=bwd_send.at[c], recv_sem=bwd_recv.at[core],
            device_id={"tm": shard - 1, "state": c}, device_id_type=MESH,
        )

    def fwd_arrival(c):
        return pltpu.make_async_remote_copy(
            src_ref=fwd_out, dst_ref=fwd_in.at[c],
            send_sem=fwd_send.at[c], recv_sem=fwd_recv.at[c],
            device_id={"state": 1 - core}, device_id_type=MESH,
        )

    def bwd_arrival(c):
        return pltpu.make_async_remote_copy(
            src_ref=bwd_out, dst_ref=bwd_in.at[c],
            send_sem=bwd_send.at[c], recv_sem=bwd_recv.at[c],
            device_id={"state": 1 - core}, device_id_type=MESH,
        )

    @pl.when(first)
    def _():
        fwd_in[0] = jnp.exp(prior_ref[...])
        fwd_in[1] = jnp.zeros((1, states), F32)

    @pl.when(last)
    def _():
        bwd_in[0] = jnp.ones((1, half), F32)
        bwd_in[1] = jnp.ones((1, half), F32)

    def forward():
        @pl.when(jnp.logical_not(first))
        def _():
            for c in range(2):
                fwd_arrival(c).wait_recv()

        @pl.when(jnp.logical_not(last))
        def _():
            v = fwd_in[0] + fwd_in[1]
            scale = 1.0 / jnp.max(v, axis=1, keepdims=True)
            mine = jnp.where(core == 0, v[:, :half], v[:, half:])
            fwd_out[...] = times(mine, chain_f[...]) * scale
            for c in range(2):
                fwd_copy(c).start()

    def backward():
        @pl.when(jnp.logical_not(last))
        def _():
            for c in range(2):
                bwd_arrival(c).wait_recv()

        @pl.when(jnp.logical_not(first))
        def _():
            w = jnp.concatenate([bwd_in[0], bwd_in[1]], axis=1)
            scale = 1.0 / jnp.max(w, axis=1, keepdims=True)
            bwd_out[...] = times(w, chain_b[...]) * scale
            for c in range(2):
                bwd_copy(c).start()

    early = shard < shard_count // 2

    @pl.when(early)
    def _():
        forward()
        backward()

    @pl.when(jnp.logical_not(early))
    def _():
        backward()
        forward()

    a = fwd_in[0] + fwd_in[1]
    a = a / jnp.max(a, axis=1, keepdims=True)
    b = jnp.concatenate([bwd_in[0], bwd_in[1]], axis=1)
    b = b / jnp.max(b, axis=1, keepdims=True)

    def walk(i, carry):
        a, b = carry
        emitted = lik[pl.ds(i, 1), :]
        scale = 1.0 / jnp.max(a, axis=1, keepdims=True)
        a_new = (a * stay + times(a, fwd_w[...])) * (emitted * scale)
        alphas[pl.ds(i, 1), :] = a_new
        t = steps - 1 - i
        betas[pl.ds(t, 1), :] = b
        x = b * lik[pl.ds(t, 1), :]
        scale = 1.0 / jnp.max(x, axis=1, keepdims=True)
        b_new = (x * stay + times(x, bwd_w[...])) * scale
        return a_new, b_new

    lax.fori_loop(0, steps, walk, (a, b))
    joint = alphas[...] * betas[...]
    factor = states / jnp.sum(joint, axis=1, keepdims=True)
    out_ref[...] = jnp.where(core == 0, joint[:, :half], joint[:, half:]) * factor

    @pl.when(jnp.logical_not(last))
    def _():
        for c in range(2):
            fwd_copy(c).wait_send()

    @pl.when(jnp.logical_not(first))
    def _():
        for c in range(2):
            bwd_copy(c).wait_send()


def shards(shard_count, observed, block_mask, jump_logit, leave_rate, emit_logit, prior_logit):
    states = jump_logit.shape[0]
    half = states // 2
    symbols = emit_logit.shape[0]
    steps = observed.shape[0]
    vmem = pl.BlockSpec(memory_space=pltpu.VMEM)
    return pl.pallas_call(
        functools.partial(kernel, shard_count),
        out_shape=jax.ShapeDtypeStruct((steps, half), F32),
        in_specs=[pl.BlockSpec(memory_space=pltpu.SMEM)] + [vmem] * 5,
        out_specs=vmem,
        scratch_shapes=[
            pltpu.VMEM((states, states), F32),
            pltpu.VMEM((states, 2 * states), BF16),
            pltpu.VMEM((states, 2 * states), BF16),
            pltpu.VMEM((symbols, states), F32),
            pltpu.VMEM((steps, states), F32),
            pltpu.VMEM((half, states), F32),
            pltpu.VMEM((half, 1), F32),
            pltpu.VMEM((half, 2 * states), BF16),
            pltpu.VMEM((states, 2 * half), BF16),
            pltpu.VMEM((1, 128), F32),
            pltpu.VMEM((1, 128), F32),
            pltpu.VMEM((1, states), F32),
            pltpu.VMEM((2, 1, states), F32),
            pltpu.VMEM((1, half), F32),
            pltpu.VMEM((2, 1, half), F32),
            pltpu.VMEM((steps, states), F32),
            pltpu.VMEM((steps, states), F32),
            pltpu.SemaphoreType.DMA((2,)),
            pltpu.SemaphoreType.DMA((2,)),
            pltpu.SemaphoreType.DMA((2,)),
            pltpu.SemaphoreType.DMA((2,)),
            pltpu.SemaphoreType.DMA((2,)),
        ],
        compiler_params=pltpu.CompilerParams(
            collective_id=0, has_side_effects=True, vmem_limit_bytes=40 * 1024 * 1024
        ),
    )(observed, block_mask, jump_logit, leave_rate[None, :], emit_logit, prior_logit[None, :])


def solution(mesh):
    return jax.shard_map(
        functools.partial(shards, mesh.shape["tm"]),
        mesh=mesh,
        in_specs=(P(("groups", "tm")), P(), P(), P(), P(), P()),
        out_specs=P(("groups", "tm"), "state"),
        check_vma=False,
    )
```

```python
import functools

import jax
import jax.numpy as jnp
from jax import lax
from jax.experimental import pallas as pl
from jax.experimental.pallas import tpu as pltpu
from jax.sharding import PartitionSpec as P

MESH = pl.DeviceIdType.MESH
F32 = jnp.float32
BF16 = jnp.bfloat16
CHUNKS = 2


def split(x):
    high = x.astype(BF16).astype(F32)
    return high, x - high


def pair(x):
    high, low = split(x)
    row = lax.broadcasted_iota(jnp.int32, (16, x.shape[1]), 0)
    return jnp.where(row == 0, high, jnp.where(row == 1, low, 0.0)).astype(BF16)


def times(x, weights):
    out = jnp.dot(pair(x), weights, preferred_element_type=F32)
    n = out.shape[1] // 2
    return (out[0:1, :n] + out[1:2, :n]) + (out[0:1, n:] + out[1:2, n:])


def put_pieces(ref, x):
    high, low = split(x)
    n = x.shape[1]
    ref[:, :n] = high.astype(BF16)
    ref[:, n:] = low.astype(BF16)


def kernel(
    shard_count,
    observed_ref, mask_ref, jump_ref, leave_ref, emit_ref, prior_ref,
    out_ref,
    moves, fwd_w, bwd_w, symbols, lik, part, logs, chain_f, chain_b,
    peak_out, peak_in, fwd_out, fwd_in, bwd_out, bwd_in, alphas, betas,
    peak_sems, fwd_send, fwd_recv, bwd_send, bwd_recv,
):
    shard = lax.axis_index("tm")
    core = lax.axis_index("state")
    states = jump_ref.shape[0]
    half = states // 2
    steps = lik.shape[0]
    first, last = shard == 0, shard == shard_count - 1

    barrier = pltpu.get_barrier_semaphore()
    pl.semaphore_signal(barrier, inc=1, device_id={"state": 1 - core}, device_id_type=MESH)

    @pl.when(jnp.logical_not(first))
    def _():
        for c in range(2):
            pl.semaphore_signal(
                barrier, inc=1, device_id={"tm": shard - 1, "state": c}, device_id_type=MESH
            )

    @pl.when(jnp.logical_not(last))
    def _():
        for c in range(2):
            pl.semaphore_signal(
                barrier, inc=1, device_id={"tm": shard + 1, "state": c}, device_id_type=MESH
            )

    width = states // mask_ref.shape[0]
    blocks = mask_ref.shape[0]
    spread = (
        lax.broadcasted_iota(jnp.int32, (states, blocks), 0) // width
        == lax.broadcasted_iota(jnp.int32, (states, blocks), 1)
    ).astype(F32).astype(BF16)
    spread_t = (
        lax.broadcasted_iota(jnp.int32, (blocks, states), 1) // width
        == lax.broadcasted_iota(jnp.int32, (blocks, states), 0)
    ).astype(F32).astype(BF16)
    eye = lax.broadcasted_iota(jnp.int32, (blocks, blocks), 0) == lax.broadcasted_iota(
        jnp.int32, (blocks, blocks), 1
    )
    grid = jnp.where(eye, 1.0, mask_ref[...].astype(F32)).astype(BF16)
    tall = jnp.dot(spread, grid, preferred_element_type=F32).astype(BF16)
    allowed = jnp.dot(tall, spread_t, preferred_element_type=F32)
    weights = jnp.where(allowed > 0.5, jnp.exp(jump_ref[...]), 0.0)
    leave = leave_ref[...]
    stay = 1.0 - leave
    leave_col = jnp.transpose(jnp.broadcast_to(leave, (128, states)))[:, 0:1]
    off = weights * (leave_col / jnp.sum(weights, axis=1, keepdims=True))
    moves[...] = off
    put_pieces(fwd_w, off)
    put_pieces(bwd_w, jnp.transpose(off))

    emit = jnp.exp(emit_ref[...])
    symbols[...] = emit
    share = 1.0 / jnp.sum(emit, axis=0, keepdims=True)
    for t in range(steps):
        lik[t:t + 1, :] = symbols[pl.ds(observed_ref[t], 1), :]
    rows = lik[...] * share
    lik[...] = rows / jnp.max(rows, axis=1, keepdims=True)

    neighbours = 1 + 2 * (
        jnp.where(first, 0, 1).astype(jnp.int32) + jnp.where(last, 0, 1).astype(jnp.int32)
    )
    pl.semaphore_wait(barrier, neighbours)

    def fwd_copy(c):
        return pltpu.make_async_remote_copy(
            src_ref=fwd_out, dst_ref=fwd_in.at[core],
            send_sem=fwd_send.at[c], recv_sem=fwd_recv.at[core],
            device_id={"tm": shard + 1, "state": c}, device_id_type=MESH,
        )

    def bwd_copy(c):
        return pltpu.make_async_remote_copy(
            src_ref=bwd_out, dst_ref=bwd_in.at[core],
            send_sem=bwd_send.at[c], recv_sem=bwd_recv.at[core],
            device_id={"tm": shard - 1, "state": c}, device_id_type=MESH,
        )

    def fwd_arrival(c):
        return pltpu.make_async_remote_copy(
            src_ref=fwd_out, dst_ref=fwd_in.at[c],
            send_sem=fwd_send.at[c], recv_sem=fwd_recv.at[c],
            device_id={"state": 1 - core}, device_id_type=MESH,
        )

    def bwd_arrival(c):
        return pltpu.make_async_remote_copy(
            src_ref=bwd_out, dst_ref=bwd_in.at[c],
            send_sem=bwd_send.at[c], recv_sem=bwd_recv.at[c],
            device_id={"state": 1 - core}, device_id_type=MESH,
        )

    def ahead(i, a):
        scale = 1.0 / jnp.max(a, axis=1, keepdims=True)
        a = (a * stay + times(a, fwd_w[...])) * (lik[pl.ds(i, 1), :] * scale)
        alphas[pl.ds(i, 1), :] = a
        return a

    def back(i, b):
        t = steps - 1 - i
        betas[pl.ds(t, 1), :] = b
        x = b * lik[pl.ds(t, 1), :]
        scale = 1.0 / jnp.max(x, axis=1, keepdims=True)
        return (x * stay + times(x, bwd_w[...])) * scale

    def opening():
        a = fwd_in[0] + fwd_in[1]
        return a / jnp.max(a, axis=1, keepdims=True)

    def closing():
        b = jnp.concatenate([bwd_in[0], bwd_in[1]], axis=1)
        return b / jnp.max(b, axis=1, keepdims=True)

    def walk_ahead():
        return lax.fori_loop(0, steps, ahead, opening())

    def walk_back():
        return lax.fori_loop(0, steps, back, closing())

    @pl.when(first)
    def _():
        fwd_in[0] = jnp.exp(prior_ref[...])
        fwd_in[1] = jnp.zeros((1, states), F32)
        fwd_out[...] = walk_ahead()
        for c in range(2):
            fwd_copy(c).start()

    @pl.when(last)
    def _():
        bwd_in[0] = jnp.ones((1, half), F32)
        bwd_in[1] = jnp.ones((1, half), F32)
        b = walk_back()
        bwd_out[...] = jnp.where(core == 0, b[:, :half], b[:, half:])
        for c in range(2):
            bwd_copy(c).start()

    @pl.when(jnp.logical_not(jnp.logical_or(first, last)))
    def _():
        own = lax.broadcasted_iota(jnp.int32, (half, states), 0) + core * half
        diagonal = own == lax.broadcasted_iota(jnp.int32, (half, states), 1)
        start = pl.multiple_of(core * half, half)
        part[...] = (moves[pl.ds(start, half), :] + jnp.where(diagonal, stay, 0.0)) * lik[0:1, :]
        logs[...] = jnp.zeros_like(logs)
        size = half // CHUNKS

        def advance(t, rescale):
            emitted = lik[pl.ds(t, 1), :]
            for h in range(CHUNKS):
                at = slice(h * size, (h + 1) * size)
                a = part[at, :]
                high, low = split(a)
                high, low = high.astype(BF16), low.astype(BF16)
                both = jnp.dot(
                    jnp.concatenate([high, low], axis=0), fwd_w[:, :states],
                    preferred_element_type=F32,
                )
                rest = jnp.dot(high, fwd_w[:, states:], preferred_element_type=F32)
                new = (a * stay + (both[:size] + (both[size:] + rest))) * emitted
                if rescale:
                    peak = jnp.max(a, axis=1, keepdims=True)
                    new = new * (1.0 / peak)
                    logs[at, :] = logs[at, :] + jnp.log(peak)
                part[at, :] = new

        def two(i, carry):
            advance(1 + 2 * i, True)
            advance(2 + 2 * i, False)
            return carry

        lax.fori_loop(0, (steps - 1) // 2, two, 0)
        if (steps - 1) % 2:
            advance(steps - 1, True)

        final_log = logs[...]
        own_peak = jnp.max(final_log + jnp.log(jnp.max(part[...], axis=1, keepdims=True)))
        peak_out[...] = jnp.full(peak_out.shape, own_peak, F32)
        peak_copy = pltpu.make_async_remote_copy(
            src_ref=peak_out, dst_ref=peak_in, send_sem=peak_sems.at[0], recv_sem=peak_sems.at[1],
            device_id={"state": 1 - core}, device_id_type=MESH,
        )
        peak_copy.start()
        peak_copy.wait()
        top = jnp.maximum(peak_out[0:1, 0:1], peak_in[0:1, 0:1])
        whole = part[...] * jnp.exp(final_log - top)
        put_pieces(chain_f, whole)
        put_pieces(chain_b, jnp.transpose(whole))

    def forward():
        @pl.when(jnp.logical_not(first))
        def _():
            for c in range(2):
                fwd_arrival(c).wait_recv()

        @pl.when(jnp.logical_not(last))
        def _():
            v = fwd_in[0] + fwd_in[1]
            scale = 1.0 / jnp.max(v, axis=1, keepdims=True)
            mine = jnp.where(core == 0, v[:, :half], v[:, half:])
            fwd_out[...] = times(mine, chain_f[...]) * scale
            for c in range(2):
                fwd_copy(c).start()

    def backward():
        @pl.when(jnp.logical_not(last))
        def _():
            for c in range(2):
                bwd_arrival(c).wait_recv()

        @pl.when(jnp.logical_not(first))
        def _():
            w = jnp.concatenate([bwd_in[0], bwd_in[1]], axis=1)
            scale = 1.0 / jnp.max(w, axis=1, keepdims=True)
            bwd_out[...] = times(w, chain_b[...]) * scale
            for c in range(2):
                bwd_copy(c).start()

    early = shard < shard_count // 2
    gap = jnp.where(early, shard_count - 1 - 2 * shard, 2 * shard - shard_count + 1)
    apart = jnp.logical_or(gap >= 3, jnp.logical_or(first, last))

    @pl.when(early)
    def _():
        @pl.when(jnp.logical_not(first))
        def _():
            forward()

            @pl.when(apart)
            def _():
                walk_ahead()

        backward()

        @pl.when(apart)
        def _():
            walk_back()

    @pl.when(jnp.logical_not(early))
    def _():
        @pl.when(jnp.logical_not(last))
        def _():
            backward()

            @pl.when(apart)
            def _():
                walk_back()

        forward()

        @pl.when(apart)
        def _():
            walk_ahead()

    @pl.when(jnp.logical_not(apart))
    def _():
        def both(i, carry):
            return ahead(i, carry[0]), back(i, carry[1])

        lax.fori_loop(0, steps, both, (opening(), closing()))

    joint = alphas[...] * betas[...]
    factor = states / jnp.sum(joint, axis=1, keepdims=True)
    out_ref[...] = jnp.where(core == 0, joint[:, :half], joint[:, half:]) * factor

    @pl.when(jnp.logical_not(last))
    def _():
        for c in range(2):
            fwd_copy(c).wait_send()

    @pl.when(jnp.logical_not(first))
    def _():
        for c in range(2):
            bwd_copy(c).wait_send()


def shards(shard_count, observed, block_mask, jump_logit, leave_rate, emit_logit, prior_logit):
    states = jump_logit.shape[0]
    half = states // 2
    symbols = emit_logit.shape[0]
    steps = observed.shape[0]
    vmem = pl.BlockSpec(memory_space=pltpu.VMEM)
    return pl.pallas_call(
        functools.partial(kernel, shard_count),
        out_shape=jax.ShapeDtypeStruct((steps, half), F32),
        in_specs=[pl.BlockSpec(memory_space=pltpu.SMEM)] + [vmem] * 5,
        out_specs=vmem,
        scratch_shapes=[
            pltpu.VMEM((states, states), F32),
            pltpu.VMEM((states, 2 * states), BF16),
            pltpu.VMEM((states, 2 * states), BF16),
            pltpu.VMEM((symbols, states), F32),
            pltpu.VMEM((steps, states), F32),
            pltpu.VMEM((half, states), F32),
            pltpu.VMEM((half, 1), F32),
            pltpu.VMEM((half, 2 * states), BF16),
            pltpu.VMEM((states, 2 * half), BF16),
            pltpu.VMEM((1, 128), F32),
            pltpu.VMEM((1, 128), F32),
            pltpu.VMEM((1, states), F32),
            pltpu.VMEM((2, 1, states), F32),
            pltpu.VMEM((1, half), F32),
            pltpu.VMEM((2, 1, half), F32),
            pltpu.VMEM((steps, states), F32),
            pltpu.VMEM((steps, states), F32),
            pltpu.SemaphoreType.DMA((2,)),
            pltpu.SemaphoreType.DMA((2,)),
            pltpu.SemaphoreType.DMA((2,)),
            pltpu.SemaphoreType.DMA((2,)),
            pltpu.SemaphoreType.DMA((2,)),
        ],
        compiler_params=pltpu.CompilerParams(
            collective_id=0, has_side_effects=True, vmem_limit_bytes=40 * 1024 * 1024
        ),
    )(observed, block_mask, jump_logit, leave_rate[None, :], emit_logit, prior_logit[None, :])


def solution(mesh):
    return jax.shard_map(
        functools.partial(shards, mesh.shape["tm"]),
        mesh=mesh,
        in_specs=(P(("groups", "tm")), P(), P(), P(), P(), P()),
        out_specs=P(("groups", "tm"), "state"),
        check_vma=False,
    )
```

```python
import functools

import jax
import jax.numpy as jnp
from jax import lax
from jax.experimental import pallas as pl
from jax.experimental.pallas import tpu as pltpu
from jax.sharding import PartitionSpec as P

MESH = pl.DeviceIdType.MESH
F32 = jnp.float32
BF16 = jnp.bfloat16
CHUNKS = 2


def split(x):
    high = x.astype(BF16).astype(F32)
    return high, x - high


def pair(x):
    high, low = split(x)
    row = lax.broadcasted_iota(jnp.int32, (16, x.shape[1]), 0)
    return jnp.where(row == 0, high, jnp.where(row == 1, low, 0.0)).astype(BF16)


def times(x, weights):
    out = jnp.dot(pair(x), weights, preferred_element_type=F32)
    n = out.shape[1] // 2
    return (out[0:1, :n] + out[1:2, :n]) + (out[0:1, n:] + out[1:2, n:])


def put_pieces(ref, x):
    high, low = split(x)
    n = x.shape[1]
    ref[:, :n] = high.astype(BF16)
    ref[:, n:] = low.astype(BF16)


def kernel(
    shard_count,
    observed_ref, mask_ref, jump_ref, leave_ref, emit_ref, prior_ref,
    out_ref,
    moves, fwd_w, bwd_w, symbols, lik, part, logs, chain_f, chain_b,
    peak_out, peak_in, fwd_out, fwd_in, bwd_out, bwd_in, alphas, betas,
    peak_sems, fwd_send, fwd_recv, bwd_send, bwd_recv,
):
    shard = lax.axis_index("tm")
    core = lax.axis_index("state")
    states = jump_ref.shape[0]
    half = states // 2
    steps = lik.shape[0]
    first, last = shard == 0, shard == shard_count - 1

    barrier = pltpu.get_barrier_semaphore()
    pl.semaphore_signal(barrier, inc=1, device_id={"state": 1 - core}, device_id_type=MESH)

    @pl.when(jnp.logical_not(first))
    def _():
        for c in range(2):
            pl.semaphore_signal(
                barrier, inc=1, device_id={"tm": shard - 1, "state": c}, device_id_type=MESH
            )

    @pl.when(jnp.logical_not(last))
    def _():
        for c in range(2):
            pl.semaphore_signal(
                barrier, inc=1, device_id={"tm": shard + 1, "state": c}, device_id_type=MESH
            )

    width = states // mask_ref.shape[0]
    blocks = mask_ref.shape[0]
    spread = (
        lax.broadcasted_iota(jnp.int32, (states, blocks), 0) // width
        == lax.broadcasted_iota(jnp.int32, (states, blocks), 1)
    ).astype(F32).astype(BF16)
    spread_t = (
        lax.broadcasted_iota(jnp.int32, (blocks, states), 1) // width
        == lax.broadcasted_iota(jnp.int32, (blocks, states), 0)
    ).astype(F32).astype(BF16)
    eye = lax.broadcasted_iota(jnp.int32, (blocks, blocks), 0) == lax.broadcasted_iota(
        jnp.int32, (blocks, blocks), 1
    )
    grid = jnp.where(eye, 1.0, mask_ref[...].astype(F32)).astype(BF16)
    tall = jnp.dot(spread, grid, preferred_element_type=F32).astype(BF16)
    allowed = jnp.dot(tall, spread_t, preferred_element_type=F32)
    weights = jnp.where(allowed > 0.5, jnp.exp(jump_ref[...]), 0.0)
    leave = leave_ref[...]
    stay = 1.0 - leave
    leave_col = jnp.transpose(jnp.broadcast_to(leave, (128, states)))[:, 0:1]
    off = weights * (leave_col / jnp.sum(weights, axis=1, keepdims=True))
    moves[...] = off
    put_pieces(fwd_w, off)
    put_pieces(bwd_w, jnp.transpose(off))

    emit = jnp.exp(emit_ref[...])
    symbols[...] = emit
    share = 1.0 / jnp.sum(emit, axis=0, keepdims=True)
    for t in range(steps):
        lik[t:t + 1, :] = symbols[pl.ds(observed_ref[t], 1), :]
    rows = lik[...] * share
    lik[...] = rows / jnp.max(rows, axis=1, keepdims=True)

    neighbours = 1 + 2 * (
        jnp.where(first, 0, 1).astype(jnp.int32) + jnp.where(last, 0, 1).astype(jnp.int32)
    )
    pl.semaphore_wait(barrier, neighbours)

    def fwd_copy(c):
        return pltpu.make_async_remote_copy(
            src_ref=fwd_out, dst_ref=fwd_in.at[core],
            send_sem=fwd_send.at[c], recv_sem=fwd_recv.at[core],
            device_id={"tm": shard + 1, "state": c}, device_id_type=MESH,
        )

    def bwd_copy(c):
        return pltpu.make_async_remote_copy(
            src_ref=bwd_out, dst_ref=bwd_in.at[core],
            send_sem=bwd_send.at[c], recv_sem=bwd_recv.at[core],
            device_id={"tm": shard - 1, "state": c}, device_id_type=MESH,
        )

    def fwd_arrival(c):
        return pltpu.make_async_remote_copy(
            src_ref=fwd_out, dst_ref=fwd_in.at[c],
            send_sem=fwd_send.at[c], recv_sem=fwd_recv.at[c],
            device_id={"state": 1 - core}, device_id_type=MESH,
        )

    def bwd_arrival(c):
        return pltpu.make_async_remote_copy(
            src_ref=bwd_out, dst_ref=bwd_in.at[c],
            send_sem=bwd_send.at[c], recv_sem=bwd_recv.at[c],
            device_id={"state": 1 - core}, device_id_type=MESH,
        )

    def ahead(i, a):
        scale = 1.0 / jnp.max(a, axis=1, keepdims=True)
        a = (a * stay + times(a, fwd_w[...])) * (lik[pl.ds(i, 1), :] * scale)
        alphas[pl.ds(i, 1), :] = a
        return a

    def back(i, b):
        t = steps - 1 - i
        betas[pl.ds(t, 1), :] = b
        x = b * lik[pl.ds(t, 1), :]
        scale = 1.0 / jnp.max(x, axis=1, keepdims=True)
        return (x * stay + times(x, bwd_w[...])) * scale

    def opening():
        a = fwd_in[0] + fwd_in[1]
        return a / jnp.max(a, axis=1, keepdims=True)

    def closing():
        b = jnp.concatenate([bwd_in[0], bwd_in[1]], axis=1)
        return b / jnp.max(b, axis=1, keepdims=True)

    def walk_ahead():
        return lax.fori_loop(0, steps, ahead, opening(), unroll=4)

    def walk_back():
        return lax.fori_loop(0, steps, back, closing(), unroll=4)

    @pl.when(first)
    def _():
        fwd_in[0] = jnp.exp(prior_ref[...])
        fwd_in[1] = jnp.zeros((1, states), F32)
        fwd_out[...] = walk_ahead()
        for c in range(2):
            fwd_copy(c).start()

    @pl.when(last)
    def _():
        bwd_in[0] = jnp.ones((1, half), F32)
        bwd_in[1] = jnp.ones((1, half), F32)
        b = walk_back()
        bwd_out[...] = jnp.where(core == 0, b[:, :half], b[:, half:])
        for c in range(2):
            bwd_copy(c).start()

    @pl.when(jnp.logical_not(jnp.logical_or(first, last)))
    def _():
        own = lax.broadcasted_iota(jnp.int32, (half, states), 0) + core * half
        diagonal = own == lax.broadcasted_iota(jnp.int32, (half, states), 1)
        start = pl.multiple_of(core * half, half)
        part[...] = (moves[pl.ds(start, half), :] + jnp.where(diagonal, stay, 0.0)) * lik[0:1, :]
        logs[...] = jnp.zeros_like(logs)
        size = half // CHUNKS

        def advance(t, rescale):
            emitted = lik[pl.ds(t, 1), :]
            for h in range(CHUNKS):
                at = slice(h * size, (h + 1) * size)
                a = part[at, :]
                high, low = split(a)
                high, low = high.astype(BF16), low.astype(BF16)
                both = jnp.dot(
                    jnp.concatenate([high, low], axis=0), fwd_w[:, :states],
                    preferred_element_type=F32,
                )
                rest = jnp.dot(high, fwd_w[:, states:], preferred_element_type=F32)
                new = (a * stay + (both[:size] + (both[size:] + rest))) * emitted
                if rescale:
                    peak = jnp.max(a, axis=1, keepdims=True)
                    new = new * (1.0 / peak)
                    logs[at, :] = logs[at, :] + jnp.log(peak)
                part[at, :] = new

        def two(i, carry):
            advance(1 + 2 * i, True)
            advance(2 + 2 * i, False)
            return carry

        lax.fori_loop(0, (steps - 1) // 2, two, 0)
        if (steps - 1) % 2:
            advance(steps - 1, True)

        final_log = logs[...]
        own_peak = jnp.max(final_log + jnp.log(jnp.max(part[...], axis=1, keepdims=True)))
        peak_out[...] = jnp.full(peak_out.shape, own_peak, F32)
        peak_copy = pltpu.make_async_remote_copy(
            src_ref=peak_out, dst_ref=peak_in, send_sem=peak_sems.at[0], recv_sem=peak_sems.at[1],
            device_id={"state": 1 - core}, device_id_type=MESH,
        )
        peak_copy.start()
        peak_copy.wait()
        top = jnp.maximum(peak_out[0:1, 0:1], peak_in[0:1, 0:1])
        whole = part[...] * jnp.exp(final_log - top)
        put_pieces(chain_f, whole)
        put_pieces(chain_b, jnp.transpose(whole))

    def forward():
        @pl.when(jnp.logical_not(first))
        def _():
            for c in range(2):
                fwd_arrival(c).wait_recv()

        @pl.when(jnp.logical_not(last))
        def _():
            v = fwd_in[0] + fwd_in[1]
            scale = 1.0 / jnp.max(v, axis=1, keepdims=True)
            mine = jnp.where(core == 0, v[:, :half], v[:, half:])
            fwd_out[...] = times(mine, chain_f[...]) * scale
            for c in range(2):
                fwd_copy(c).start()

    def backward():
        @pl.when(jnp.logical_not(last))
        def _():
            for c in range(2):
                bwd_arrival(c).wait_recv()

        @pl.when(jnp.logical_not(first))
        def _():
            w = jnp.concatenate([bwd_in[0], bwd_in[1]], axis=1)
            scale = 1.0 / jnp.max(w, axis=1, keepdims=True)
            bwd_out[...] = times(w, chain_b[...]) * scale
            for c in range(2):
                bwd_copy(c).start()

    early = shard < shard_count // 2
    gap = jnp.where(early, shard_count - 1 - 2 * shard, 2 * shard - shard_count + 1)
    apart = jnp.logical_or(gap >= 3, jnp.logical_or(first, last))

    @pl.when(early)
    def _():
        @pl.when(jnp.logical_not(first))
        def _():
            forward()

            @pl.when(apart)
            def _():
                walk_ahead()

        backward()

        @pl.when(apart)
        def _():
            walk_back()

    @pl.when(jnp.logical_not(early))
    def _():
        @pl.when(jnp.logical_not(last))
        def _():
            backward()

            @pl.when(apart)
            def _():
                walk_back()

        forward()

        @pl.when(apart)
        def _():
            walk_ahead()

    @pl.when(jnp.logical_not(apart))
    def _():
        def both(i, carry):
            return ahead(i, carry[0]), back(i, carry[1])

        lax.fori_loop(0, steps, both, (opening(), closing()))

    joint = alphas[...] * betas[...]
    factor = states / jnp.sum(joint, axis=1, keepdims=True)
    out_ref[...] = jnp.where(core == 0, joint[:, :half], joint[:, half:]) * factor

    @pl.when(jnp.logical_not(last))
    def _():
        for c in range(2):
            fwd_copy(c).wait_send()

    @pl.when(jnp.logical_not(first))
    def _():
        for c in range(2):
            bwd_copy(c).wait_send()


def shards(shard_count, observed, block_mask, jump_logit, leave_rate, emit_logit, prior_logit):
    states = jump_logit.shape[0]
    half = states // 2
    symbols = emit_logit.shape[0]
    steps = observed.shape[0]
    vmem = pl.BlockSpec(memory_space=pltpu.VMEM)
    return pl.pallas_call(
        functools.partial(kernel, shard_count),
        out_shape=jax.ShapeDtypeStruct((steps, half), F32),
        in_specs=[pl.BlockSpec(memory_space=pltpu.SMEM)] + [vmem] * 5,
        out_specs=vmem,
        scratch_shapes=[
            pltpu.VMEM((states, states), F32),
            pltpu.VMEM((states, 2 * states), BF16),
            pltpu.VMEM((states, 2 * states), BF16),
            pltpu.VMEM((symbols, states), F32),
            pltpu.VMEM((steps, states), F32),
            pltpu.VMEM((half, states), F32),
            pltpu.VMEM((half, 1), F32),
            pltpu.VMEM((half, 2 * states), BF16),
            pltpu.VMEM((states, 2 * half), BF16),
            pltpu.VMEM((1, 128), F32),
            pltpu.VMEM((1, 128), F32),
            pltpu.VMEM((1, states), F32),
            pltpu.VMEM((2, 1, states), F32),
            pltpu.VMEM((1, half), F32),
            pltpu.VMEM((2, 1, half), F32),
            pltpu.VMEM((steps, states), F32),
            pltpu.VMEM((steps, states), F32),
            pltpu.SemaphoreType.DMA((2,)),
            pltpu.SemaphoreType.DMA((2,)),
            pltpu.SemaphoreType.DMA((2,)),
            pltpu.SemaphoreType.DMA((2,)),
            pltpu.SemaphoreType.DMA((2,)),
        ],
        compiler_params=pltpu.CompilerParams(
            collective_id=0, has_side_effects=True, vmem_limit_bytes=40 * 1024 * 1024
        ),
    )(observed, block_mask, jump_logit, leave_rate[None, :], emit_logit, prior_logit[None, :])


def solution(mesh):
    return jax.shard_map(
        functools.partial(shards, mesh.shape["tm"]),
        mesh=mesh,
        in_specs=(P(("groups", "tm")), P(), P(), P(), P(), P()),
        out_specs=P(("groups", "tm"), "state"),
        check_vma=False,
    )
```

```python
import functools

import jax
import jax.numpy as jnp
from jax import lax
from jax.experimental import pallas as pl
from jax.experimental.pallas import tpu as pltpu
from jax.sharding import PartitionSpec as P

MESH = pl.DeviceIdType.MESH
F32 = jnp.float32
BF16 = jnp.bfloat16
CHUNKS = 2


def split(x):
    high = x.astype(BF16).astype(F32)
    return high, x - high


def pair(x):
    high, low = split(x)
    row = lax.broadcasted_iota(jnp.int32, (16, x.shape[1]), 0)
    return jnp.where(row == 0, high, jnp.where(row == 1, low, 0.0)).astype(BF16)


def times(x, weights):
    out = jnp.dot(pair(x), weights, preferred_element_type=F32)
    n = out.shape[1] // 2
    return (out[0:1, :n] + out[1:2, :n]) + (out[0:1, n:] + out[1:2, n:])


def put_pieces(ref, x):
    high, low = split(x)
    n = x.shape[1]
    ref[:, :n] = high.astype(BF16)
    ref[:, n:] = low.astype(BF16)


def kernel(
    shard_count,
    observed_ref, mask_ref, jump_ref, leave_ref, emit_ref, prior_ref,
    out_ref,
    moves, fwd_w, bwd_w, symbols, lik, part, logs, chain_f, chain_b,
    peak_out, peak_in, fwd_out, fwd_in, bwd_out, bwd_in, alphas, betas,
    peak_sems, fwd_send, fwd_recv, bwd_send, bwd_recv,
):
    shard = lax.axis_index("tm")
    core = lax.axis_index("state")
    states = jump_ref.shape[0]
    half = states // 2
    steps = lik.shape[0]
    first, last = shard == 0, shard == shard_count - 1

    barrier = pltpu.get_barrier_semaphore()
    pl.semaphore_signal(barrier, inc=1, device_id={"state": 1 - core}, device_id_type=MESH)

    @pl.when(jnp.logical_not(first))
    def _():
        for c in range(2):
            pl.semaphore_signal(
                barrier, inc=1, device_id={"tm": shard - 1, "state": c}, device_id_type=MESH
            )

    @pl.when(jnp.logical_not(last))
    def _():
        for c in range(2):
            pl.semaphore_signal(
                barrier, inc=1, device_id={"tm": shard + 1, "state": c}, device_id_type=MESH
            )

    width = states // mask_ref.shape[0]
    blocks = mask_ref.shape[0]
    spread = (
        lax.broadcasted_iota(jnp.int32, (states, blocks), 0) // width
        == lax.broadcasted_iota(jnp.int32, (states, blocks), 1)
    ).astype(F32).astype(BF16)
    spread_t = (
        lax.broadcasted_iota(jnp.int32, (blocks, states), 1) // width
        == lax.broadcasted_iota(jnp.int32, (blocks, states), 0)
    ).astype(F32).astype(BF16)
    eye = lax.broadcasted_iota(jnp.int32, (blocks, blocks), 0) == lax.broadcasted_iota(
        jnp.int32, (blocks, blocks), 1
    )
    grid = jnp.where(eye, 1.0, mask_ref[...].astype(F32)).astype(BF16)
    tall = jnp.dot(spread, grid, preferred_element_type=F32).astype(BF16)
    allowed = jnp.dot(tall, spread_t, preferred_element_type=F32)
    weights = jnp.where(allowed > 0.5, jnp.exp(jump_ref[...]), 0.0)
    leave = leave_ref[...]
    stay = 1.0 - leave
    leave_col = jnp.transpose(jnp.broadcast_to(leave, (128, states)))[:, 0:1]
    off = weights * (leave_col / jnp.sum(weights, axis=1, keepdims=True))
    moves[...] = off
    put_pieces(fwd_w, off)
    put_pieces(bwd_w, jnp.transpose(off))

    emit = jnp.exp(emit_ref[...])
    symbols[...] = emit
    share = 1.0 / jnp.sum(emit, axis=0, keepdims=True)
    for t in range(steps):
        lik[t:t + 1, :] = symbols[pl.ds(observed_ref[t], 1), :]
    rows = lik[...] * share
    lik[...] = rows / jnp.max(rows, axis=1, keepdims=True)

    neighbours = 1 + 2 * (
        jnp.where(first, 0, 1).astype(jnp.int32) + jnp.where(last, 0, 1).astype(jnp.int32)
    )
    pl.semaphore_wait(barrier, neighbours)

    def fwd_copy(c):
        return pltpu.make_async_remote_copy(
            src_ref=fwd_out, dst_ref=fwd_in.at[core],
            send_sem=fwd_send.at[c], recv_sem=fwd_recv.at[core],
            device_id={"tm": shard + 1, "state": c}, device_id_type=MESH,
        )

    def bwd_copy(c):
        return pltpu.make_async_remote_copy(
            src_ref=bwd_out, dst_ref=bwd_in.at[core],
            send_sem=bwd_send.at[c], recv_sem=bwd_recv.at[core],
            device_id={"tm": shard - 1, "state": c}, device_id_type=MESH,
        )

    def fwd_arrival(c):
        return pltpu.make_async_remote_copy(
            src_ref=fwd_out, dst_ref=fwd_in.at[c],
            send_sem=fwd_send.at[c], recv_sem=fwd_recv.at[c],
            device_id={"state": 1 - core}, device_id_type=MESH,
        )

    def bwd_arrival(c):
        return pltpu.make_async_remote_copy(
            src_ref=bwd_out, dst_ref=bwd_in.at[c],
            send_sem=bwd_send.at[c], recv_sem=bwd_recv.at[c],
            device_id={"state": 1 - core}, device_id_type=MESH,
        )

    def ahead(i, a):
        scale = 1.0 / jnp.max(a, axis=1, keepdims=True)
        a = (a * stay + times(a, fwd_w[...])) * (lik[pl.ds(i, 1), :] * scale)
        alphas[pl.ds(i, 1), :] = a
        return a

    def back(i, b):
        t = steps - 1 - i
        betas[pl.ds(t, 1), :] = b
        x = b * lik[pl.ds(t, 1), :]
        scale = 1.0 / jnp.max(x, axis=1, keepdims=True)
        return (x * stay + times(x, bwd_w[...])) * scale

    def opening():
        a = fwd_in[0] + fwd_in[1]
        return a / jnp.max(a, axis=1, keepdims=True)

    def closing():
        b = jnp.concatenate([bwd_in[0], bwd_in[1]], axis=1)
        return b / jnp.max(b, axis=1, keepdims=True)

    def walk_ahead():
        return lax.fori_loop(0, steps, ahead, opening(), unroll=4)

    def walk_back():
        return lax.fori_loop(0, steps, back, closing(), unroll=4)

    @pl.when(first)
    def _():
        fwd_in[0] = jnp.exp(prior_ref[...])
        fwd_in[1] = jnp.zeros((1, states), F32)
        fwd_out[...] = walk_ahead()
        for c in range(2):
            fwd_copy(c).start()

    @pl.when(last)
    def _():
        bwd_in[0] = jnp.ones((1, half), F32)
        bwd_in[1] = jnp.ones((1, half), F32)
        b = walk_back()
        bwd_out[...] = jnp.where(core == 0, b[:, :half], b[:, half:])
        for c in range(2):
            bwd_copy(c).start()

    @pl.when(jnp.logical_not(jnp.logical_or(first, last)))
    def _():
        own = lax.broadcasted_iota(jnp.int32, (half, states), 0) + core * half
        diagonal = own == lax.broadcasted_iota(jnp.int32, (half, states), 1)
        start = pl.multiple_of(core * half, half)
        part[...] = (moves[pl.ds(start, half), :] + jnp.where(diagonal, stay, 0.0)) * lik[0:1, :]
        logs[...] = jnp.zeros_like(logs)
        size = half // CHUNKS

        def advance(t, rescale):
            emitted = lik[pl.ds(t, 1), :]
            for h in range(CHUNKS):
                at = slice(h * size, (h + 1) * size)
                a = part[at, :]
                high, low = split(a)
                high, low = high.astype(BF16), low.astype(BF16)
                both = jnp.dot(
                    jnp.concatenate([high, low], axis=0), fwd_w[:, :states],
                    preferred_element_type=F32,
                )
                rest = jnp.dot(high, fwd_w[:, states:], preferred_element_type=F32)
                new = (a * stay + (both[:size] + (both[size:] + rest))) * emitted
                if rescale:
                    peak = jnp.max(a, axis=1, keepdims=True)
                    new = new * (1.0 / peak)
                    logs[at, :] = logs[at, :] + jnp.log(peak)
                part[at, :] = new

        def two(i, carry):
            advance(1 + 2 * i, True)
            advance(2 + 2 * i, False)
            return carry

        lax.fori_loop(0, (steps - 1) // 2, two, 0, unroll=3)
        if (steps - 1) % 2:
            advance(steps - 1, True)

        final_log = logs[...]
        own_peak = jnp.max(final_log + jnp.log(jnp.max(part[...], axis=1, keepdims=True)))
        peak_out[...] = jnp.full(peak_out.shape, own_peak, F32)
        peak_copy = pltpu.make_async_remote_copy(
            src_ref=peak_out, dst_ref=peak_in, send_sem=peak_sems.at[0], recv_sem=peak_sems.at[1],
            device_id={"state": 1 - core}, device_id_type=MESH,
        )
        peak_copy.start()
        peak_copy.wait()
        top = jnp.maximum(peak_out[0:1, 0:1], peak_in[0:1, 0:1])
        whole = part[...] * jnp.exp(final_log - top)
        put_pieces(chain_f, whole)
        put_pieces(chain_b, jnp.transpose(whole))

    def forward():
        @pl.when(jnp.logical_not(first))
        def _():
            for c in range(2):
                fwd_arrival(c).wait_recv()

        @pl.when(jnp.logical_not(last))
        def _():
            v = fwd_in[0] + fwd_in[1]
            scale = 1.0 / jnp.max(v, axis=1, keepdims=True)
            mine = jnp.where(core == 0, v[:, :half], v[:, half:])
            fwd_out[...] = times(mine, chain_f[...]) * scale
            for c in range(2):
                fwd_copy(c).start()

    def backward():
        @pl.when(jnp.logical_not(last))
        def _():
            for c in range(2):
                bwd_arrival(c).wait_recv()

        @pl.when(jnp.logical_not(first))
        def _():
            w = jnp.concatenate([bwd_in[0], bwd_in[1]], axis=1)
            scale = 1.0 / jnp.max(w, axis=1, keepdims=True)
            bwd_out[...] = times(w, chain_b[...]) * scale
            for c in range(2):
                bwd_copy(c).start()

    early = shard < shard_count // 2
    gap = jnp.where(early, shard_count - 1 - 2 * shard, 2 * shard - shard_count + 1)
    apart = jnp.logical_or(gap >= 3, jnp.logical_or(first, last))

    @pl.when(early)
    def _():
        @pl.when(jnp.logical_not(first))
        def _():
            forward()

            @pl.when(apart)
            def _():
                walk_ahead()

        backward()

        @pl.when(apart)
        def _():
            walk_back()

    @pl.when(jnp.logical_not(early))
    def _():
        @pl.when(jnp.logical_not(last))
        def _():
            backward()

            @pl.when(apart)
            def _():
                walk_back()

        forward()

        @pl.when(apart)
        def _():
            walk_ahead()

    @pl.when(jnp.logical_not(apart))
    def _():
        def both(i, carry):
            return ahead(i, carry[0]), back(i, carry[1])

        lax.fori_loop(0, steps, both, (opening(), closing()))

    joint = alphas[...] * betas[...]
    factor = states / jnp.sum(joint, axis=1, keepdims=True)
    out_ref[...] = jnp.where(core == 0, joint[:, :half], joint[:, half:]) * factor

    @pl.when(jnp.logical_not(last))
    def _():
        for c in range(2):
            fwd_copy(c).wait_send()

    @pl.when(jnp.logical_not(first))
    def _():
        for c in range(2):
            bwd_copy(c).wait_send()


def shards(shard_count, observed, block_mask, jump_logit, leave_rate, emit_logit, prior_logit):
    states = jump_logit.shape[0]
    half = states // 2
    symbols = emit_logit.shape[0]
    steps = observed.shape[0]
    vmem = pl.BlockSpec(memory_space=pltpu.VMEM)
    return pl.pallas_call(
        functools.partial(kernel, shard_count),
        out_shape=jax.ShapeDtypeStruct((steps, half), F32),
        in_specs=[pl.BlockSpec(memory_space=pltpu.SMEM)] + [vmem] * 5,
        out_specs=vmem,
        scratch_shapes=[
            pltpu.VMEM((states, states), F32),
            pltpu.VMEM((states, 2 * states), BF16),
            pltpu.VMEM((states, 2 * states), BF16),
            pltpu.VMEM((symbols, states), F32),
            pltpu.VMEM((steps, states), F32),
            pltpu.VMEM((half, states), F32),
            pltpu.VMEM((half, 1), F32),
            pltpu.VMEM((half, 2 * states), BF16),
            pltpu.VMEM((states, 2 * half), BF16),
            pltpu.VMEM((1, 128), F32),
            pltpu.VMEM((1, 128), F32),
            pltpu.VMEM((1, states), F32),
            pltpu.VMEM((2, 1, states), F32),
            pltpu.VMEM((1, half), F32),
            pltpu.VMEM((2, 1, half), F32),
            pltpu.VMEM((steps, states), F32),
            pltpu.VMEM((steps, states), F32),
            pltpu.SemaphoreType.DMA((2,)),
            pltpu.SemaphoreType.DMA((2,)),
            pltpu.SemaphoreType.DMA((2,)),
            pltpu.SemaphoreType.DMA((2,)),
            pltpu.SemaphoreType.DMA((2,)),
        ],
        compiler_params=pltpu.CompilerParams(
            collective_id=0, has_side_effects=True, vmem_limit_bytes=40 * 1024 * 1024
        ),
    )(observed, block_mask, jump_logit, leave_rate[None, :], emit_logit, prior_logit[None, :])


def solution(mesh):
    return jax.shard_map(
        functools.partial(shards, mesh.shape["tm"]),
        mesh=mesh,
        in_specs=(P(("groups", "tm")), P(), P(), P(), P(), P()),
        out_specs=P(("groups", "tm"), "state"),
        check_vma=False,
    )
```
